32 devices in a mesh: walk: 8 (over z, x), elec: 2 (over y), chol: 2 (over core).
Axes of the slice: x: 2, y: 2, z: 4, core: 2. Of those that a mesh axis runs over, the one named last changes fastest.
Arguments:
- green: bfloat16 [8, 1024, 256], P('walk'), may hold values from -6 to 6
- chol_vecs: bfloat16 [16, 256, 1024], P(('walk', 'chol'), 'elec'), may hold values from -0.3125 to 0.3125
Outputs:
- gradient: float32 [8, 1024, 256], P('walk', ('elec', 'chol'))
The draws below stay inside these ranges and needn't reach their ends.
All inputs are finite; a program needn't handle non-finite values.
Results may differ from the reference program's by a relative error of at most 0.0029.
Values may be sent and summed in bfloat16 or wider, within the bound.
A program may use at most 64 MiB of HBM per device.

```python
import jax
import jax.numpy as jnp
from jax import lax

NORB = 1024
NE = 256
NCHOL = 16
NW = 8


def block_scale(key, shape, cuts, low, high):
    level = 1.0
    for axis_at, blocks in cuts:
        steps = jax.random.uniform(jax.random.fold_in(jax.random.fold_in(key, 6), axis_at), (blocks,), jnp.float32, low / len(cuts), high / len(cuts))
        level = level * jnp.repeat(jnp.exp(steps), shape[axis_at] // blocks).reshape((-1,) + (1,) * (len(shape) - 1 - axis_at))
    return level


def noise(rng, dims, width, bound, shards=(), held_as=jnp.bfloat16):
    values = jax.random.normal(rng, dims, jnp.float32) * width
    if len(shards) > 0:
        values = block_scale(rng, dims, shards, -0.22, 0.18) * values
    return jnp.clip(values, min=-bound, max=bound).astype(held_as)


def setup_inputs(seed: int = 0) -> dict:
    keys = jax.random.split(jax.random.key(seed), 3)
    green = noise(keys[0], (NW, NORB, NE), 1.0, 6.0, ((0, 8),))
    chol_vecs = noise(keys[1], (NCHOL, NE, NORB), ((NCHOL * NE * NORB) ** -0.25), 0.3125, ((0, 16), (1, 2)))
    return {"green": green, "chol_vecs": chol_vecs}


def reference(green, chol_vecs):
    green_wide = green.astype(jnp.float32)

    def absorb_one(running, block):
        block_wide = block.astype(jnp.float32)
        intersection = jnp.einsum('ap,wpb->wab', block_wide, green_wide)
        intersection = lax.optimization_barrier(intersection.astype(jnp.bfloat16)).astype(jnp.float32)
        running = running - jnp.einsum('ap,wba->wpb', block_wide, intersection)
        return running, None

    gradient, unused = lax.scan(absorb_one, jnp.zeros(green.shape, jnp.float32), chol_vecs)
    return gradient
```

```python
import functools

import jax
import jax.numpy as jnp
from jax import lax
from jax.experimental import pallas as pl
from jax.experimental.pallas import tpu as pltpu
from jax.sharding import PartitionSpec as P

F32 = jnp.float32
BF16 = jnp.bfloat16


def kernel(n, green, own, out, cholesky, greens, parts, sums_in, sums_out,
           l_send, l_recv, g_send, g_recv, s_send, s_recv, own_sem):
    walk, elec, chol = (lax.axis_index(name) for name in ("walk", "elec", "chol"))
    line = n // 2
    z, x = walk // 2, lax.rem(walk, 2)
    rows, orbitals = own.shape
    quarter = orbitals // 4
    sets = cholesky.shape[0]
    to_x, to_elec, to_chol = {"walk": 2 * z + 1 - x}, {"elec": 1 - elec}, {"chol": 1 - chol}

    def at(place):
        return {"walk": 2 * place + x}

    def others(visit):
        @pl.loop(0, 2 * (line - 1))
        def _(event):
            way, k = lax.rem(event, 2), event // 2
            place = jnp.where(way == 0, line - 1 - k, k)
            pl.when(jnp.where(way == 0, place > z, place < z))(lambda: visit(way, place))

    barrier = pltpu.get_barrier_semaphore()

    def greet(device):
        pl.semaphore_signal(barrier, inc=1, device_id=device, device_id_type=pl.DeviceIdType.MESH)

    for device in (to_x, to_elec, to_chol):
        greet(device)
    others(lambda way, place: greet(at(place)))

    def block(x_at, elec_at):
        return cholesky.at[2 * x_at + chol, pl.ds(pl.multiple_of(elec_at * rows, rows), rows)]

    def strip(elec_at):
        return pl.ds(pl.multiple_of((2 * elec_at + chol) * quarter, quarter), quarter)

    mine = pltpu.make_async_copy(own, block(x, elec), own_sem.at[0])
    mine.start()
    home = pltpu.make_async_copy(green, greens.at[z], own_sem.at[1])
    home.start()

    def remote(source, target, send, recv, device):
        return pltpu.make_async_remote_copy(
            src_ref=source, dst_ref=target, send_sem=send, recv_sem=recv,
            device_id=device, device_id_type=pl.DeviceIdType.MESH)

    def move(i, source, target, device):
        return remote(source, target, l_send.at[i], l_recv.at[i], device)

    own_elec = move(0, own, block(x, elec), to_elec)
    own_x = move(1, own, block(x, elec), to_x)
    own_chol = move(2, own, block(x, elec), to_chol)
    elec_x = move(3, block(x, 1 - elec), block(x, 1 - elec), to_x)
    elec_chol = move(4, block(x, 1 - elec), block(x, 1 - elec), to_chol)
    x_chol = move(5, block(1 - x, elec), block(1 - x, elec), to_chol)
    far_chol = move(6, block(1 - x, 1 - elec), block(1 - x, 1 - elec), to_chol)

    def launch(place):
        return remote(green.at[strip(elec)], greens.at[z, strip(elec)],
                      g_send.at[0, place], g_recv.at[0, z], at(place))

    def spread(kind, place):
        region = greens.at[place, strip(1 - elec if kind == 3 else elec)]
        return remote(region, region, g_send.at[kind, place], g_recv.at[kind, place],
                      to_elec if kind == 1 else to_chol)

    def arrival(place):
        region = greens.at[place, strip(elec)]
        return remote(region, region, g_send.at[0, place], g_recv.at[0, place], at(place))

    pl.semaphore_wait(barrier, line + 2)
    own_elec.start()
    own_x.start()
    others(lambda way, place: launch(place).start())
    own_chol.start()

    own_elec.wait_recv()
    elec_x.start()
    elec_chol.start()

    def pass_on(way, place):
        arrival(place).wait_recv()
        spread(1, place).start()
        spread(2, place).start()

    others(pass_on)
    own_x.wait_recv()
    x_chol.start()

    def pass_over(way, place):
        spread(1, place).wait_recv()
        spread(3, place).start()

    elec_x.wait_recv()
    far_chol.start()
    others(pass_over)
    for copy in (own_chol, elec_chol, x_chol, far_chol):
        copy.wait_recv()
    mine.wait()
    home.wait()

    columns = pl.ds(pl.multiple_of((2 * elec + chol) * quarter, quarter), quarter)

    def contribution(place):
        total = None
        for g in range(sets):
            intersection = jnp.dot(cholesky[g], greens[place], preferred_element_type=F32).astype(BF16)
            term = jnp.dot(intersection, cholesky[g, :, columns], preferred_element_type=F32)
            total = term if total is None else total + term
        return total

    def step(way, place):
        return remote(sums_out.at[way, place], sums_in.at[way, place], s_send.at[way, place],
                      s_recv.at[way, place], at(jnp.where(way == 0, z + 1, z - 1)))

    def add(way, place):
        sums = remote(sums_out.at[way, place], sums_in.at[way, place], s_send.at[way, place],
                      s_recv.at[way, place], to_x)
        sums.wait_recv()
        parts[...] += sums_in[way, place].astype(F32)

    def reduce(way, place):
        spread(2, place).wait_recv()
        spread(3, place).wait_recv()
        parts[...] = contribution(place)
        pl.when(jnp.where(way == 0, z > 0, z < line - 1))(lambda: add(way, place))
        sums_out[way, place] = parts[...].astype(BF16)
        step(way, place).start()

    others(reduce)
    parts[...] = contribution(z)
    pl.when(z > 0)(lambda: add(0, z))
    pl.when(z < line - 1)(lambda: add(1, z))
    out[...] = -parts[...].T

    for copy in (own_elec, own_x, own_chol, elec_x, elec_chol, x_chol, far_chol):
        copy.wait_send()

    def finish(way, place):
        launch(place).wait_send()
        for kind in (1, 2, 3):
            spread(kind, place).wait_send()
        step(way, place).wait_send()

    others(finish)


def shards(n, green, chol_vecs):
    orbitals, electrons = green.shape[1:]
    rows = chol_vecs.shape[1]
    line = n // 2
    quarter = orbitals // 4
    hbm = pl.BlockSpec(memory_space=pltpu.HBM)
    dma = pltpu.SemaphoreType.DMA
    gradient = pl.pallas_call(
        functools.partial(kernel, n),
        out_shape=jax.ShapeDtypeStruct((quarter, electrons), F32),
        in_specs=[hbm, hbm],
        out_specs=pl.BlockSpec(memory_space=pltpu.VMEM),
        scratch_shapes=[
            pltpu.VMEM((4, 2 * rows, orbitals), BF16),
            pltpu.VMEM((line, orbitals, electrons), BF16),
            pltpu.VMEM((electrons, quarter), F32),
            pltpu.VMEM((2, line, electrons, quarter), BF16),
            pltpu.VMEM((2, line, electrons, quarter), BF16),
            dma((7,)), dma((7,)),
            dma((4, line)), dma((4, line)),
            dma((2, line)), dma((2, line)),
            dma((2,)),
        ],
        compiler_params=pltpu.CompilerParams(
            collective_id=0, has_side_effects=True, vmem_limit_bytes=48 * 1024 * 1024),
    )(green[0], chol_vecs[0])
    return gradient[None]


def solution(mesh):
    in_specs = (P("walk", None, None), P(("walk", "chol"), "elec", None))
    out_specs = P("walk", ("elec", "chol"), None)
    return jax.shard_map(functools.partial(shards, mesh.shape["walk"]), mesh=mesh,
                         in_specs=in_specs, out_specs=out_specs, check_vma=False)
```
